256 devices in a mesh: owner: 128 (over z, y, x), replica: 2 (over core).
Axes of the slice: x: 4, y: 4, z: 8, core: 2. Of those that a mesh axis runs over, the one named last changes fastest.
Arguments:
- queries: bfloat16 [24576, 8192], P(('owner', 'replica')), may hold values from -200 to 200
- suffix_kv: bfloat16 [24576, 32, 1024], P(('owner', 'replica')), may hold values from -6 to 6
- suffix_len: int32 [24576], P(('owner', 'replica')), may hold values from 2 to 32, as said below
- row_prefix: int32 [24576, 1], P(('owner', 'replica')), may hold values from 0 to 127; in each aligned block of 96 rows (0 to 95, 96 to 191, ...) at most 2 rows name the same one
- prefix_owner: int32 [128], replicated, may hold values from 0 to 127, each once
- prefix_kv: bfloat16 [128, 2, 512, 1024], P('owner', 'replica'), may hold values from -6 to 6
- missing_pages: int32 [128, 2, 1], P('owner'), may hold values from 0 to 3, as said below
Outputs:
- attended: bfloat16 [24576, 8192], P(('owner', 'replica'))
The draws below stay inside these ranges and needn't reach their ends.
Inputs may be any that keep to these rules, and one draw needn't show every extreme that they name: `row_prefix`: in the rows of one device no prefix appears more than 2 times, and in some device's rows one prefix appears exactly 2 times. `prefix_owner`: each owner index appears once. `missing_pages`: for each owner the lists of its two copies hold 2 distinct pages; a page listed for one copy is zero in that copy and present in the other. `suffix_len`: row 0 has 32 live tokens.
All inputs are finite; a program needn't handle non-finite values.
Results may differ from the reference program's by a relative error of at most 0.0056.
Values may be sent and summed in bfloat16 or wider, within the bound.
A program may use at most 128 MiB of HBM per device.

```python
import math
import jax
import jax.numpy as jnp
import numpy as np
from jax import lax

HQ = 64
KVH = 4
HD = 128
ROW_DEV = 96
SUF = 32
PLEN = 512
PAGE = 128
CAP = 2
PAGES = 4
MISS = 1
PREFIXES = 128
ROWS = 24576


def missing_lists(key):
    subkeys = jax.random.split(jax.random.fold_in(key, 9), PREFIXES)
    orders = jax.vmap(lambda subkey: jax.random.permutation(subkey, PAGES))(subkeys)
    return orders[:, :2 * MISS].reshape(PREFIXES, 2, MISS).astype(jnp.int32)


def draw_missing_pages(key, part):
    return missing_lists(key)


def draw_prefix_kv(key, part):
    page_lists = missing_lists(key)
    key = jax.random.fold_in(key, 21)
    row_width = 2 * KVH * HD
    drawn = jnp.clip(jax.random.normal(key, (PREFIXES, PLEN, row_width), jnp.float32), -6.0, 6.0)
    page_index = jnp.arange(PLEN) // PAGE
    absent = jnp.any(page_index[None, None, :, None] == page_lists[:, :, None, :], axis=-1)
    return jnp.where(absent[..., None], 0.0, drawn[:, None]).astype(jnp.bfloat16)


def draw_suffix_kv(key, part):
    key = jax.random.fold_in(key, 31)
    row_width = 2 * KVH * HD
    drawn = jnp.clip(jax.random.normal(key, (ROWS, SUF, row_width), jnp.float32), -6.0, 6.0)
    return drawn.astype(jnp.bfloat16)


def draw_suffix_len(key, part):
    key = jax.random.fold_in(key, 51)
    lengths = jax.random.randint(key, (ROWS,), 2, SUF + 1)
    return jnp.where(jnp.arange(ROWS) == 0, SUF, lengths).astype(jnp.int32)


def draw_queries(key, part):
    key = jax.random.fold_in(key, 41)
    drawn = jnp.clip(jax.random.normal(key, (ROWS, HQ, HD), jnp.float32), -6.0, 6.0)
    return drawn.reshape(ROWS, HQ * HD).astype(jnp.bfloat16)


def assign_block(key, own, number, rows, count, top, reach, lean):
    ranking = jax.random.permutation(key, count)
    heavy_load, usual = portions_of(count, rows * top, reach, lean, True), portions_of(count, rows * top, reach, lean, False)
    places = jnp.arange(count)

    def named(tallies, turn):
        used = int((tallies > 0).sum())
        fixed = max(1, used // 4)
        moved = fixed + (places - fixed + turn * (used - fixed)) % max(1, count - fixed)
        return jnp.zeros((count,), jnp.int32).at[ranking[jnp.where(places < fixed, places, moved)]].set(jnp.asarray(tallies, jnp.int32))

    tallies = jnp.where(number % 4 == 0, named(heavy_load, number // 4), named(usual, number - number // 4 - 1))
    mixed = jax.random.permutation(jax.random.fold_in(own, 3), count)
    giver, receiver = mixed[0:count // 2 * 2:2], mixed[1:count // 2 * 2:2]
    room = jnp.minimum(tallies[giver] - 1, reach - tallies[receiver]) // 2
    room = jnp.where((giver == ranking[0]) | (receiver == ranking[0]) | (tallies[receiver] == 0), 0, jnp.maximum(room, 0))
    moved = jax.random.randint(jax.random.fold_in(own, 4), (count // 2,), 0, 1 << 20) % (room + 1)
    tallies = tallies.at[giver].add(-moved).at[receiver].add(moved)
    labels = jnp.searchsorted(jnp.cumsum(tallies), jnp.arange(rows * top), side="right").astype(jnp.int32)
    table = labels.reshape(top, rows).T
    table = table[jax.random.permutation(jax.random.fold_in(own, 1), rows)]
    turn = jax.random.randint(jax.random.fold_in(own, 2), (rows, 1), 0, top)
    return jnp.take_along_axis(table, (jnp.arange(top)[None, :] + turn) % top, axis=1)


def portions_of(count, total, limit, skew, full):
    loads = [(1 << 20) // math.isqrt(grade ** skew) + 1 for grade in range(1, count + 1)]
    largest = limit if full else min(limit, max(-(-total // count), total * loads[0] // sum(loads)))
    least = 1 if total - largest >= count - 1 else 0
    counts, spare = [largest] + [least] * (count - 1), total - largest - least * (count - 1)
    while spare > 0:
        movable = [i for i in range(1, count) if counts[i] < largest] or [i for i in range(1, count) if counts[i] < limit]
        mass, remaining = sum([loads[i] for i in movable]), spare
        for i in movable:
            addition = min(limit - counts[i], max(1, remaining * loads[i] // mass), spare)
            counts[i] = counts[i] + addition
            spare = spare - addition
    return np.array(counts)


def setup_inputs(seed: int = 0) -> dict:
    key_of = jax.random.split(jax.random.key(seed), 8)
    queries = draw_queries(jax.random.fold_in(key_of[7], 71), 0)
    suffix_kv = draw_suffix_kv(jax.random.fold_in(key_of[7], 71), 0)
    suffix_len = draw_suffix_len(jax.random.fold_in(key_of[7], 71), 0)
    row_prefix_keys = jax.random.split(jax.random.fold_in(key_of[3], 1), ROWS // ROW_DEV)
    row_prefix_turns = jax.random.permutation(jax.random.fold_in(key_of[3], 3), ROWS // ROW_DEV)
    row_prefix = jax.vmap(lambda own, number: assign_block(jax.random.fold_in(key_of[3], 2), own, number, ROW_DEV, PREFIXES, 1, CAP, 2))(row_prefix_keys, row_prefix_turns).reshape((ROWS, 1))
    prefix_owner = jax.random.permutation(key_of[4], PREFIXES).astype(jnp.int32)
    prefix_kv = draw_prefix_kv(jax.random.fold_in(key_of[7], 71), 0)
    missing_pages = draw_missing_pages(jax.random.fold_in(key_of[7], 71), 0)
    return dict(queries=queries, suffix_kv=suffix_kv, suffix_len=suffix_len, row_prefix=row_prefix, prefix_owner=prefix_owner, prefix_kv=prefix_kv, missing_pages=missing_pages)


def cache_partial(query_rows, cache):
    count = query_rows.shape[0]
    group_size = HQ // KVH
    grouped = query_rows.reshape(count, KVH, group_size, HD).astype(jnp.float32)
    key_rows = cache[:, :KVH * HD].reshape(-1, KVH, HD).astype(jnp.float32)
    value_rows = cache[:, KVH * HD:].reshape(-1, KVH, HD).astype(jnp.float32)
    scores = jnp.einsum('sgqd,tgd->sgqt', grouped, key_rows) * (HD ** -0.5)
    maxima = jnp.max(scores, axis=-1)
    expd = jnp.exp(scores - maxima[..., None])
    totals = jnp.sum(expd, axis=-1)
    weights = lax.optimization_barrier(expd.astype(jnp.bfloat16)).astype(jnp.float32)
    outputs = jnp.einsum('sgqt,tgd->sgqd', weights, value_rows) / totals[..., None]
    return maxima.reshape(count, HQ), totals.reshape(count, HQ), outputs.astype(jnp.bfloat16).reshape(count, HQ * HD)


def suffix_partial(query_rows, suffix_rows, lengths):
    count = query_rows.shape[0]
    span = suffix_rows.shape[1]
    group_size = HQ // KVH
    grouped = query_rows.reshape(count, KVH, group_size, HD).astype(jnp.float32)
    key_rows = suffix_rows[:, :, :KVH * HD].reshape(count, span, KVH, HD).astype(jnp.float32)
    value_rows = suffix_rows[:, :, KVH * HD:].reshape(count, span, KVH, HD).astype(jnp.float32)
    scores = jnp.einsum('rgqd,rtgd->rgqt', grouped, key_rows) * (HD ** -0.5)
    valid = jnp.arange(span)[None, None, None, :] < lengths[:, None, None, None]
    maxima = jnp.max(jnp.where(valid, scores, -jnp.inf), axis=-1)
    expd = jnp.where(valid, jnp.exp(scores - maxima[..., None]), 0.0)
    totals = jnp.sum(expd, axis=-1)
    weights = lax.optimization_barrier(expd.astype(jnp.bfloat16)).astype(jnp.float32)
    outputs = jnp.einsum('rgqt,rtgd->rgqd', weights, value_rows) / totals[..., None]
    return maxima.reshape(count, HQ), totals.reshape(count, HQ), outputs.reshape(count, HQ, HD)


def merge_parts(pre_max, pre_tot, pre_out, suf_max, suf_tot, suf_out):
    count = suf_out.shape[0]
    top = jnp.maximum(pre_max, suf_max)
    first = jnp.exp(pre_max - top) * pre_tot
    second = jnp.exp(suf_max - top) * suf_tot
    prefix_part = pre_out.astype(jnp.float32).reshape(count, HQ, HD)
    mixed = (first[..., None] * prefix_part + second[..., None] * suf_out) / (first + second)[..., None]
    return mixed.reshape(count, HQ * HD).astype(jnp.bfloat16)


def reference(queries, suffix_kv, suffix_len, row_prefix, prefix_owner, prefix_kv, missing_pages):
    page_index = jnp.arange(PLEN) // PAGE
    absent = jnp.any(page_index[None, :, None] == missing_pages[:, 0][:, None, :], axis=-1)
    caches = jnp.where(absent[..., None], prefix_kv[:, 1], prefix_kv[:, 0])
    hits = row_prefix[:, 0][:, None] == jnp.arange(PREFIXES)[None, :]
    owner_of = jnp.sum(jnp.where(hits, prefix_owner[None, :], 0), axis=1).astype(jnp.int32)

    def one_row(items):
        query_row, suffix_row, length, holder = items
        cache = lax.dynamic_index_in_dim(caches, holder, 0, keepdims=False)
        pre_max, pre_tot, pre_out = cache_partial(query_row[None], cache)
        suf_max, suf_tot, suf_out = suffix_partial(query_row[None], suffix_row[None], length[None])
        return merge_parts(pre_max, pre_tot, pre_out, suf_max, suf_tot, suf_out)[0]

    return lax.map(one_row, (queries, suffix_kv, suffix_len, owner_of))
```

```python
import functools

import jax
import jax.numpy as jnp
from jax import lax
from jax.experimental import pallas as pl
from jax.experimental.pallas import tpu as pltpu
from jax.sharding import PartitionSpec as P

HQ = 64
KVH = 4
HD = 128
PAGE = 128
GROUP = HQ // KVH
NZ, NY, NX = 8, 4, 4
PLANE = NY * NX
SLOTS = 2 * NZ
SCALE = HD**-0.5
SCALE2 = SCALE * 1.4426950408889634
MESH = pl.DeviceIdType.MESH

ORDER = (
    ((0, 0), (1, 1), (3, 3), (1, 3)),
    ((3, 1), (2, 1), (1, 2), (1, 0)),
    ((3, 0), (0, 1), (0, 3), (2, 0)),
    ((0, 2), (2, 3), (3, 2), (2, 2)),
)
CHUNKS = tuple(
    tuple(2 * (dy * NX + dx) + hh for dx, dy in chunk for hh in (0, 1)) for chunk in ORDER
)
PLACE = {i: (c, n) for c, chunk in enumerate(CHUNKS) for n, i in enumerate(chunk)}


def fused_kernel(
    cap,
    idx_ref, row_ref, miss_ref, meta_hbm, live_ref, q_hbm, suf_hbm, kv_hbm,
    out_ref,
    q, suf, kv, kvp, cache, tx, rx0, rx1, rx2, rx3, obuf, otx, orx, stx, srx, mrx, tab, sufo, lses, apad,
    in_sem, core_send, core_recv, z_send, z_recv,
    q_send, q_recv, m_send, m_recv, tab_sem, o_send, o_recv, s_send, s_recv,
):
    own = lax.axis_index("owner")
    core = lax.axis_index("replica")
    rx = (rx0, rx1, rx2, rx3)
    z, y, x = own // PLANE, own // NX % NY, own % NX
    here = own % PLANE

    def plane(dx, dy):
        return ((y + dy) % NY) * NX + (x + dx) % NX

    def other(i, sign):
        cell, hh = i // 2, i % 2
        dx, dy = cell % NX, cell // NX
        spot = z * PLANE + plane(sign * dx + NX, sign * dy + NY)
        return spot, (1 - core if hh else core)

    load_kv = pltpu.make_async_copy(kv_hbm, kv, in_sem.at[0])
    load_q = pltpu.make_async_copy(q_hbm, q, in_sem.at[1])
    load_suf = pltpu.make_async_copy(suf_hbm, suf, in_sem.at[2])
    load_kv.start()
    load_q.start()
    load_suf.start()

    z_up = (z + 1) % NZ * PLANE + here
    z_down = (z + NZ - 1) % NZ * PLANE + here
    barrier = pltpu.get_barrier_semaphore()
    for i in range(1, 2 * PLANE):
        pl.semaphore_signal(barrier, inc=1, device_id=other(i, 1), device_id_type=MESH)
    for spot in (z_up, z_down):
        pl.semaphore_signal(barrier, inc=1, device_id=(spot, core), device_id_type=MESH)
    pl.semaphore_wait(barrier, 2 * PLANE + 1)

    load_kv.wait()
    swaps = []
    for part in range(2):
        lanes = pl.ds(pl.multiple_of(part * 512 + (1 - core) * 256, 256), 256)
        swap = pltpu.make_async_remote_copy(
            src_ref=kv.at[:, lanes], dst_ref=kvp.at[part],
            send_sem=core_send.at[part], recv_sem=core_recv.at[part],
            device_id=(own, 1 - core), device_id_type=MESH,
        )
        swap.start()
        swaps.append(swap)

    load_q.wait()
    q_copies, m_copies = {}, {}

    def send_queries(i):
        cell, hh = i // 2, i % 2
        dest = plane(cell % NX, cell // NX)
        first = pl.multiple_of((1 - core if hh else core) * 32, 32)
        arrive = rx[PLACE[i][0]].at[PLACE[i][1]]
        into = arrive if i == 0 else tx.at[i]

        def put(j, carry):
            into[j] = q[idx_ref[dest * cap + j], pl.ds(first, 32), :]
            return carry

        lax.fori_loop(0, cap, put, 0, unroll=True)
        if i == 0:
            copy = pltpu.make_async_copy(meta_hbm.at[dest], mrx.at[0], m_recv.at[0])
            copy.start()
            m_copies[0] = copy
            return
        copy = pltpu.make_async_remote_copy(
            src_ref=meta_hbm.at[dest], dst_ref=mrx.at[i],
            send_sem=m_send.at[i], recv_sem=m_recv.at[i],
            device_id=other(i, 1), device_id_type=MESH,
        )
        copy.start()
        m_copies[i] = copy
        copy = pltpu.make_async_remote_copy(
            src_ref=tx.at[i], dst_ref=arrive,
            send_sem=q_send.at[i], recv_sem=q_recv.at[i],
            device_id=other(i, 1), device_id_type=MESH,
        )
        copy.start()
        q_copies[i] = copy

    for i in CHUNKS[0]:
        send_queries(i)

    for swap in swaps:
        swap.wait_recv()
    for part in range(2):
        lanes = pl.ds(pl.multiple_of(part * 512 + core * 256, 256), 256)
        for page in range(4):
            rows = slice(page * PAGE, (page + 1) * PAGE)
            take = jnp.where(page == miss_ref[0], 1 - core, core)
            pick = jnp.full((PAGE, 256), take, jnp.int32) == 1
            cache[0, part, rows, :] = jnp.where(pick, kvp[part, rows, :], kv[rows, lanes])

    def ring(step, up):
        if step < 3:
            src = cache.at[step if up or step == 0 else 4 + step]
            dst = cache.at[step + 1 if up else 5 + step]
        elif up:
            src, dst = cache.at[3, 0], cache.at[4, 0]
        else:
            src, dst = cache.at[7, 1], cache.at[4, 1]
        way = 0 if up else 1
        return pltpu.make_async_remote_copy(
            src_ref=src, dst_ref=dst, send_sem=z_send.at[way, step], recv_sem=z_recv.at[way, step],
            device_id=(z_up if up else z_down, core), device_id_type=MESH,
        )

    rings = [[ring(step, up) for up in (True, False)] for step in range(4)]
    for hop in rings[0]:
        hop.start()
    for chunk in CHUNKS[1:]:
        for i in chunk:
            send_queries(i)

    load_suf.wait()

    def suffix_block(b, carry):
        col = lax.broadcasted_iota(jnp.int32, (128, 256), 1)
        row = lax.broadcasted_iota(jnp.int32, (128, 256), 0)
        valid = (col // 32 == row // GROUP) & (
            jnp.broadcast_to(live_ref[b], (128, 256)) > 0.0
        )
        lane = lax.broadcasted_iota(jnp.int32, (128, 128), 1)
        head = lax.broadcasted_iota(jnp.int32, (128, 128), 0) % GROUP
        rows = pl.ds(b * 8, 8)
        stat = jnp.zeros((8, 128), jnp.float32)
        ones = jnp.ones((256, 128), jnp.bfloat16)
        for g in range(KVH):
            qs = q[rows, g * GROUP : (g + 1) * GROUP, :].reshape(128, HD)
            ks = suf[rows, :, g * HD : (g + 1) * HD].reshape(256, HD)
            vs = suf[rows, :, 512 + g * HD : 512 + (g + 1) * HD].reshape(256, HD)
            s = lax.dot_general(qs, ks, (((1,), (1,)), ((), ())), preferred_element_type=jnp.float32)
            s = jnp.where(valid, s, -3e38)
            top = jnp.max(s, axis=1, keepdims=True)
            w = jnp.exp2((s - top) * SCALE2).astype(jnp.bfloat16)
            o = jnp.dot(w, jnp.concatenate([vs, ones], axis=1), preferred_element_type=jnp.float32)
            total = o[:, HD:]
            sufo[rows, g * GROUP : (g + 1) * GROUP, :] = (o[:, :HD] / total).reshape(8, GROUP, HD)
            lse = top * SCALE + jnp.log(total)
            spread = jnp.where(lane == g * GROUP + head, lse, 0.0)
            stat = stat + jnp.sum(spread.reshape(8, GROUP, 128), axis=1)
        lses[pl.ds(pl.multiple_of(b * 8, 8), 8), :] = stat
        return carry

    for step in range(3):
        lax.fori_loop(step * 4, step * 4 + 4, suffix_block, 0)
        for hop in rings[step]:
            hop.wait_recv()
        for hop in rings[step + 1]:
            hop.start()
    for hop in rings[3]:
        hop.wait_recv()

    o_copies, s_copies = {}, {}
    ones = jnp.ones((512, 128), jnp.bfloat16)
    lane = lax.broadcasted_iota(jnp.int32, (256, 128), 1)
    within = lax.broadcasted_iota(jnp.int32, (256, 128), 0) % 32
    for number, chunk in enumerate(CHUNKS):
        tabs = []
        for i in chunk:
            m_copies[i].wait_recv() if i else m_copies[i].wait()
            fetch = pltpu.make_async_copy(mrx.at[i], tab.at[i], tab_sem.at[i])
            fetch.start()
            tabs.append(fetch)
        for i in chunk:
            if i:
                q_copies[i].wait_recv()
        for fetch in tabs:
            fetch.wait()

        def prefix_block(s, carry, number=number, chunk=chunk):
            p = (z + jnp.where(s < 5, NZ - s, s - 4)) % NZ
            stat = jnp.zeros((8, 128), jnp.float32)
            for g in range(2):
                heads = slice(g * GROUP, (g + 1) * GROUP)
                qs = jnp.concatenate(
                    [
                        rx[number][n, tab[i, 0, 2 * p + k], heads, :]
                        for n, i in enumerate(chunk)
                        for k in range(2)
                    ],
                    axis=0,
                )
                ks = cache[s, 0, :, g * HD : (g + 1) * HD]
                vs = cache[s, 1, :, g * HD : (g + 1) * HD]
                sc = lax.dot_general(
                    qs, ks, (((1,), (1,)), ((), ())), preferred_element_type=jnp.float32
                )
                top = jnp.max(sc, axis=1, keepdims=True)
                w = jnp.exp2((sc - top) * SCALE2).astype(jnp.bfloat16)
                o = jnp.dot(w, jnp.concatenate([vs, ones], axis=1), preferred_element_type=jnp.float32)
                total = o[:, HD:]
                res = (o[:, :HD] / total).astype(jnp.bfloat16)
                for n in range(8):
                    for k in range(2):
                        at = (2 * n + k) * GROUP
                        obuf[n, 2 * p + k, heads, :] = res[at : at + GROUP]
                lse = top * SCALE + jnp.log(total)
                spot = within // GROUP * 64 + core * 32 + g * GROUP + within % GROUP
                spread = jnp.where(lane == spot, lse, 0.0)
                stat = stat + jnp.sum(spread.reshape(8, 32, 128), axis=1)
            for n, i in enumerate(chunk):
                stx[i, pl.ds(p, 1), :] = stat[n : n + 1]
            return carry

        lax.fori_loop(0, NZ, prefix_block, 0)
        for n, i in enumerate(chunk):
            into = orx if i == 0 else otx

            def pack(j, carry, n=n, i=i, into=into):
                into[i, j] = obuf[n, tab[i, 1, j]]
                return carry

            lax.fori_loop(0, cap, pack, 0, unroll=True)
            if i == 0:
                srx[0] = stx[0]
                continue
            copy = pltpu.make_async_remote_copy(
                src_ref=stx.at[i], dst_ref=srx.at[i], send_sem=s_send.at[i], recv_sem=s_recv.at[i],
                device_id=other(i, -1), device_id_type=MESH,
            )
            copy.start()
            s_copies[i] = copy
            copy = pltpu.make_async_remote_copy(
                src_ref=otx.at[i], dst_ref=orx.at[i], send_sem=o_send.at[i], recv_sem=o_recv.at[i],
                device_id=other(i, -1), device_id_type=MESH,
            )
            copy.start()
            o_copies[i] = copy

    for chunk in CHUNKS:
        for i in chunk:
            if i:
                s_copies[i].wait_recv()
                o_copies[i].wait_recv()

    for b in range(12):
        rows = []
        for r in range(8 * b, 8 * b + 8):
            cell, slot = row_ref[0, r], row_ref[2, r]
            pair = srx[2 * cell, pl.ds(slot // 2, 1), :] + srx[2 * cell + 1, pl.ds(slot // 2, 1), :]
            rows.append(jnp.where(jnp.full((1, 128), slot % 2, jnp.int32) == 1, pltpu.roll(pair, 64, 1), pair))
        apad[8 * b : 8 * b + 8, :] = jnp.concatenate(rows, axis=0)
    share = 1.0 / (1.0 + jnp.exp(lses[...] - apad[0:96, :]))
    apad[0:96, :] = share
    apad[96:128, :] = jnp.zeros((32, 128), jnp.float32)
    turned = jnp.transpose(apad[...])
    for r in range(96):
        cell, j = row_ref[0, r], row_ref[1, r]
        pre = jnp.concatenate([orx[2 * cell + core, j], orx[2 * cell + 1 - core, j]], axis=0)
        mine = sufo[r]
        weight = jnp.broadcast_to(turned[:HQ, r : r + 1], (HQ, HD))
        out_ref[r] = (mine + weight * (pre.astype(jnp.float32) - mine)).astype(jnp.bfloat16)

    for swap in swaps:
        swap.wait_send()
    for pair in rings:
        for hop in pair:
            hop.wait_send()
    for group in (q_copies, o_copies, s_copies):
        for copy in group.values():
            copy.wait_send()
    for i, copy in m_copies.items():
        if i:
            copy.wait_send()


def routes(prefix_rows, owner_table, cap):
    rows = prefix_rows.shape[0]
    hits = prefix_rows[:, None] == jnp.arange(owner_table.shape[0], dtype=jnp.int32)[None, :]
    owner_of = jnp.sum(jnp.where(hits, owner_table[None, :], 0), axis=1)
    spot, level = owner_of % PLANE, owner_of // PLANE
    earlier = jnp.arange(rows)[None, :] < jnp.arange(rows)[:, None]
    same_owner = owner_of[:, None] == owner_of[None, :]
    slot = level * 2 + jnp.sum((same_owner & earlier).astype(jnp.int32), axis=1)
    same_spot = spot[:, None] == spot[None, :]
    rank = jnp.sum((same_spot & earlier).astype(jnp.int32), axis=1)
    to_spot = spot[None, :] == jnp.arange(PLANE, dtype=jnp.int32)[:, None]
    at_rank = rank[None, :] == jnp.arange(16, dtype=jnp.int32)[:, None]
    at_slot = slot[None, :] == jnp.arange(SLOTS, dtype=jnp.int32)[:, None]
    by_rank = to_spot[:, None, :] & at_rank[None, :, :]
    by_slot = to_spot[:, None, :] & at_slot[None, :, :]
    index = jnp.sum(jnp.where(by_rank, jnp.arange(rows, dtype=jnp.int32), 0), axis=-1)
    slot_at = jnp.sum(jnp.where(by_rank, slot, 0), axis=-1)
    rank_at = jnp.sum(jnp.where(by_slot & (rank < cap), rank, 0), axis=-1)
    own = lax.axis_index("owner")
    dx = (spot % NX - own % NX) % NX
    dy = (spot // NX - own // NX) % NY
    row_table = jnp.stack([dy * NX + dx, jnp.minimum(rank, cap - 1), slot])
    meta = jnp.zeros((PLANE, 8, 128), jnp.int32).at[:, 0, :SLOTS].set(rank_at).at[:, 1, :16].set(slot_at)
    return index[:, :cap].reshape(-1), row_table, meta


def fused(cap, index, row_table, missing, meta, live, queries, suffix_kv, own_copy):
    count = queries.shape[0]
    smem = pl.BlockSpec(memory_space=pltpu.SMEM)
    vmem = pl.BlockSpec(memory_space=pltpu.VMEM)
    hbm = pl.BlockSpec(memory_space=pl.ANY)
    n = 2 * PLANE
    dma = pltpu.SemaphoreType.DMA
    bf16, f32 = jnp.bfloat16, jnp.float32
    return pl.pallas_call(
        functools.partial(fused_kernel, cap),
        out_shape=jax.ShapeDtypeStruct((count, HQ, HD), bf16),
        in_specs=[smem, smem, smem, hbm, vmem, hbm, hbm, hbm],
        out_specs=vmem,
        scratch_shapes=[
            pltpu.VMEM((count, HQ, HD), bf16),
            pltpu.VMEM((count, 32, 1024), bf16),
            pltpu.VMEM((512, 1024), bf16),
            pltpu.VMEM((2, 512, 256), bf16),
            pltpu.VMEM((NZ, 2, 512, 256), bf16),
            pltpu.VMEM((n, cap, 32, HD), bf16),
            *[pltpu.VMEM((8, cap, 32, HD), bf16) for _ in CHUNKS],
            pltpu.VMEM((8, SLOTS, 32, HD), bf16),
            pltpu.VMEM((n, cap, 32, HD), bf16),
            pltpu.VMEM((n, cap, 32, HD), bf16),
            pltpu.VMEM((n, 8, 128), f32),
            pltpu.VMEM((n, 8, 128), f32),
            pltpu.VMEM((n, 8, 128), jnp.int32),
            pltpu.SMEM((n, 8, 128), jnp.int32),
            pltpu.VMEM((count, HQ, HD), f32),
            pltpu.VMEM((count, 128), f32),
            pltpu.VMEM((128, 128), f32),
            dma((3,)), dma((2,)), dma((2,)), dma((2, 4)), dma((2, 4)),
            dma((n,)), dma((n,)), dma((n,)), dma((n,)), dma((n,)),
            dma((n,)), dma((n,)), dma((n,)), dma((n,)),
        ],
        compiler_params=pltpu.CompilerParams(
            collective_id=cap, has_side_effects=True, vmem_limit_bytes=58 * 2**20
        ),
    )(index, row_table, missing, meta, live, queries, suffix_kv, own_copy)


def body(queries, suffix_kv, suffix_len, row_prefix, prefix_owner, prefix_kv, missing_pages):
    count, width = queries.shape
    index, row_table, meta = routes(row_prefix[:, 0], prefix_owner, 16)
    live = (jnp.arange(32, dtype=jnp.int32)[None, :] < suffix_len[:, None]).astype(jnp.float32)
    out = fused(
        16, index, row_table, missing_pages[0, 0], meta, live.reshape(count // 8, 1, 256),
        queries.reshape(count, HQ, HD), suffix_kv, prefix_kv[0, 0],
    )
    return out.reshape(count, width)


def solution(mesh):
    in_specs = (
        P(("owner", "replica"), None),
        P(("owner", "replica"), None, None),
        P(("owner", "replica")),
        P(("owner", "replica"), None),
        P(),
        P("owner", "replica", None, None),
        P("owner", None, None),
    )
    out_specs = P(("owner", "replica"), None)
    return jax.shard_map(body, mesh=mesh, in_specs=in_specs, out_specs=out_specs, check_vma=False)
```

```python
import functools

import jax
import jax.numpy as jnp
from jax import lax
from jax.experimental import pallas as pl
from jax.experimental.pallas import tpu as pltpu
from jax.sharding import PartitionSpec as P

HQ = 64
KVH = 4
HD = 128
PAGE = 128
GROUP = HQ // KVH
NZ, NY, NX = 8, 4, 4
PLANE = NY * NX
SLOTS = 2 * NZ
SCALE = HD**-0.5
SCALE2 = SCALE * 1.4426950408889634
MESH = pl.DeviceIdType.MESH

ORDER = (
    ((0, 0), (1, 1), (3, 3), (1, 3)),
    ((3, 1), (2, 1), (1, 2), (1, 0)),
    ((3, 0), (0, 1), (0, 3), (2, 0)),
    ((0, 2), (2, 3), (3, 2), (2, 2)),
)
CHUNKS = tuple(
    tuple(2 * (dy * NX + dx) + hh for dx, dy in chunk for hh in (0, 1)) for chunk in ORDER
)
PLACE = {i: (c, n) for c, chunk in enumerate(CHUNKS) for n, i in enumerate(chunk)}


def work(t):
    chunk = jnp.where(t < 5, 0, jnp.where(t < 10, 1, jnp.where(t < 12, 0, jnp.where(t < 14, 1, jnp.where(
        t < 21, 2, jnp.where(t < 28, 3, t - 28))))))
    place = jnp.where(t < 5, t, jnp.where(t < 12, t - 5, jnp.where(t < 14, t - 7, jnp.where(
        t < 21, t - 14, jnp.where(t < 28, t - 21, 7)))))
    return chunk, place


def fused_kernel(
    cap,
    pre_ref, own_ref, len_ref, miss_ref, q_hbm, suf_hbm, kv_hbm,
    out_ref, over_ref,
    q, suf, kv, kvp, cache, tx, rx0, rx1, rx2, rx3, rbuf, obuf, otx, orx, stx, srx,
    rows_v, tab_v, mrx, flag_v, frx, tab, sufo, lses, apad,
    in_sem, core_send, core_recv, z_send, z_recv,
    q_send, q_recv, m_send, m_recv, tab_sem, o_send, o_recv, s_send, s_recv,
    f_send, f_recv,
):
    own = lax.axis_index("owner")
    core = lax.axis_index("replica")
    rx = (rx0, rx1, rx2, rx3)
    z, y, x = own // PLANE, own // NX % NY, own % NX
    here = own % PLANE

    def plane(dx, dy):
        return ((y + dy) % NY) * NX + (x + dx) % NX

    def other(i, sign):
        cell, hh = i // 2, i % 2
        dx, dy = cell % NX, cell // NX
        spot = z * PLANE + plane(sign * dx + NX, sign * dy + NY)
        return spot, (1 - core if hh else core)

    load_kv = pltpu.make_async_copy(kv_hbm, kv, in_sem.at[0])
    load_q = pltpu.make_async_copy(q_hbm, q, in_sem.at[1])
    load_suf = pltpu.make_async_copy(suf_hbm, suf, in_sem.at[2])
    load_kv.start()
    load_q.start()

    z_up = (z + 1) % NZ * PLANE + here
    z_down = (z + NZ - 1) % NZ * PLANE + here
    barrier = pltpu.get_barrier_semaphore()
    for i in range(1, 2 * PLANE):
        pl.semaphore_signal(barrier, inc=1, device_id=other(i, 1), device_id_type=MESH)
    for dz in range(1, NZ):
        level = ((z + dz) % NZ * PLANE + here, core)
        pl.semaphore_signal(barrier, inc=1, device_id=level, device_id_type=MESH)

    lane = lax.broadcasted_iota(jnp.int32, (128, 128), 1)
    sub = lax.broadcasted_iota(jnp.int32, (128, 128), 0)

    def down(row):
        return jnp.transpose(jnp.broadcast_to(row, (128, 128)))

    def pick(mask, value):
        return jnp.sum(jnp.where(mask, value, 0), axis=0, keepdims=True)

    count = pre_ref.shape[1]
    rows_v[...] = jnp.full((8, 128), -1, jnp.int32)
    rows_v[0:1, 0:count] = pre_ref[...]
    real = lane[0:1] < count
    owner = pick(sub == rows_v[0:1, :], down(own_ref[...]))
    spot = jnp.where(real, owner & 15, 99)
    owner = jnp.where(real, owner, 999)
    earlier = sub < lane
    repeat = pick((down(owner) == owner) & earlier, 1)
    slot = jnp.minimum((owner >> 4) * 2 + repeat, SLOTS - 1)
    rank = pick((down(spot) == spot) & earlier, 1)
    kept = jnp.minimum(rank, cap - 1)
    by_rank, by_slot = down(spot * 16 + rank), down(spot * 16 + slot)
    slot_down, kept_down = down(slot), down(kept)
    for half in range(2):
        keys = lane + 128 * half
        tab_v[half : half + 1, :] = jnp.minimum(pick(by_rank == keys, sub), count - 1)
        tab_v[2 + half : 3 + half, :] = jnp.minimum(pick(by_rank == keys, slot_down), SLOTS - 1)
        tab_v[4 + half : 5 + half, :] = jnp.minimum(pick(by_slot == keys, kept_down), cap - 1)
    cell = (((spot >> 2) - y) & 3) * 4 + (((spot & 3) - x) & 3)
    tab_v[6:7, :] = cell * 256 + kept * 16 + slot
    tab_v[7:8, :] = jnp.where(real & (rank >= cap), 1, 0)
    load_tab = pltpu.make_async_copy(tab_v, tab.at[0], tab_sem.at[0])
    load_tab.start()
    load_kv.wait()
    pl.semaphore_wait(barrier, 2 * PLANE + NZ - 2)

    swaps = []
    for part in range(2):
        lanes = pl.ds(pl.multiple_of(part * 512 + (1 - core) * 256, 256), 256)
        swap = pltpu.make_async_remote_copy(
            src_ref=kv.at[:, lanes], dst_ref=kvp.at[part],
            send_sem=core_send.at[part], recv_sem=core_recv.at[part],
            device_id=(own, 1 - core), device_id_type=MESH,
        )
        swap.start()
        swaps.append(swap)

    q_copies, m_copies = {}, {}

    def send_table(i):
        copy = pltpu.make_async_remote_copy(
            src_ref=tab_v, dst_ref=mrx.at[i], send_sem=m_send.at[i], recv_sem=m_recv.at[i],
            device_id=other(i, 1), device_id_type=MESH,
        )
        copy.start()
        m_copies[i] = copy

    def send_queries(i):
        cell, hh = i // 2, i % 2
        dest = plane(cell % NX, cell // NX)
        first = pl.multiple_of((1 - core if hh else core) * 32, 32)
        arrive = rx[PLACE[i][0]].at[PLACE[i][1]]
        into = arrive if i == 0 else tx.at[i]

        def put(j, carry):
            into[j] = q[tab[0, dest // 8, dest % 8 * 16 + j], pl.ds(first, 32), :]
            return carry

        lax.fori_loop(0, cap, put, 0, unroll=True)
        if i == 0:
            return
        copy = pltpu.make_async_remote_copy(
            src_ref=tx.at[i], dst_ref=arrive,
            send_sem=q_send.at[i], recv_sem=q_recv.at[i],
            device_id=other(i, 1), device_id_type=MESH,
        )
        copy.start()
        q_copies[i] = copy

    load_q.wait()
    load_suf.start()
    load_tab.wait()
    for i in range(1, 2 * PLANE):
        send_table(i)
    for i in CHUNKS[0]:
        send_queries(i)

    def ring(step, up, part):
        if step < 3:
            src = cache.at[step if up or step == 0 else 4 + step, part]
            dst = cache.at[step + 1 if up else 5 + step, part]
        else:
            src, dst = cache.at[3 if up else 7, part], cache.at[4, part]
        way = 0 if up else 1
        return pltpu.make_async_remote_copy(
            src_ref=src, dst_ref=dst,
            send_sem=z_send.at[way, step, part], recv_sem=z_recv.at[way, step, part],
            device_id=(z_up if up else z_down, core), device_id_type=MESH,
        )

    rings = [
        [[ring(step, up, part) for up in (True, False) if step < 3 or up == (part == 0)] for part in range(2)]
        for step in range(4)
    ]

    def turn(step):
        for part in range(2):
            for hop in rings[step][part]:
                hop.wait_recv()
            if step < 3:
                for hop in rings[step + 1][part]:
                    hop.start()

    for part in range(2):
        swaps[part].wait_recv()
        lanes = pl.ds(pl.multiple_of(part * 512 + core * 256, 256), 256)
        for page in range(4):
            rows = slice(page * PAGE, (page + 1) * PAGE)
            take = jnp.where(page == miss_ref[0], 1 - core, core)
            pick_it = jnp.full((PAGE, 256), take, jnp.int32) == 1
            cache[0, part, rows, :] = jnp.where(pick_it, kvp[part, rows, :], kv[rows, lanes])
        for hop in rings[0][part]:
            hop.start()
    for chunk in CHUNKS[1:]:
        for i in chunk:
            send_queries(i)

    load_suf.wait()

    def suffix_block(b, carry):
        col = lax.broadcasted_iota(jnp.int32, (GROUP, 256), 1)
        valid = jnp.concatenate(
            [(col >= 32 * n) & (col < 32 * n + len_ref[b * 8 + n]) for n in range(8)], axis=0
        )
        head = sub % GROUP
        rows = pl.ds(b * 8, 8)
        stat = jnp.zeros((8, 128), jnp.float32)
        ones = jnp.ones((256, 128), jnp.bfloat16)
        for g in range(KVH):
            qs = q[rows, g * GROUP : (g + 1) * GROUP, :].reshape(128, HD)
            ks = suf[rows, :, g * HD : (g + 1) * HD].reshape(256, HD)
            vs = suf[rows, :, 512 + g * HD : 512 + (g + 1) * HD].reshape(256, HD)
            s = lax.dot_general(qs, ks, (((1,), (1,)), ((), ())), preferred_element_type=jnp.float32)
            s = jnp.where(valid, s, -3e38)
            top = jnp.max(s, axis=1, keepdims=True)
            w = jnp.exp2((s - top) * SCALE2).astype(jnp.bfloat16)
            o = jnp.dot(w, jnp.concatenate([vs, ones], axis=1), preferred_element_type=jnp.float32)
            total = o[:, HD:]
            sufo[rows, g * GROUP : (g + 1) * GROUP, :] = (o[:, :HD] / total).reshape(8, GROUP, HD)
            lse = top * SCALE + jnp.log(total)
            spread = jnp.where(lane == g * GROUP + head, lse, 0.0)
            stat = stat + jnp.sum(spread.reshape(8, GROUP, 128), axis=1)
        lses[pl.ds(pl.multiple_of(b * 8, 8), 8), :] = stat
        return carry

    lax.fori_loop(0, count // 8, suffix_block, 0)
    turn(0)

    flags = tab_v[...]
    for i in range(1, 2 * PLANE):
        m_copies[i].wait_recv()
        flags = jnp.maximum(flags, mrx[i])
    flag_v[...] = flags
    f_copies = []
    for dz in range(1, NZ):
        copy = pltpu.make_async_remote_copy(
            src_ref=flag_v, dst_ref=frx.at[dz - 1], send_sem=f_send.at[dz - 1], recv_sem=f_recv.at[dz - 1],
            device_id=((z + dz) % NZ * PLANE + here, core), device_id_type=MESH,
        )
        copy.start()
        f_copies.append(copy)

    base, row = here % 8 * 16, here // 8
    ones = jnp.ones((512, 128), jnp.bfloat16)
    lane2 = lax.broadcasted_iota(jnp.int32, (256, 128), 1)
    within = lax.broadcasted_iota(jnp.int32, (256, 128), 0) % 32
    spot2 = within // GROUP * 64 + core * 32 + within % GROUP

    def arrive(number):
        chunk = CHUNKS[number]
        tabs = []
        for i in chunk:
            if i:
                fetch = pltpu.make_async_copy(mrx.at[i], tab.at[i], tab_sem.at[i])
                fetch.start()
                tabs.append(fetch)
        for i in chunk:
            if i:
                q_copies[i].wait_recv()
        for fetch in tabs:
            fetch.wait()
        for n, i in enumerate(chunk):

            def spread_out(s, carry, n=n, i=i):
                rbuf[8 * number + n, s] = rx[number][n, tab[i, 4 + row, base + s]]
                return carry

            lax.fori_loop(0, SLOTS, spread_out, 0, unroll=True)

    def step(t, carry):
        c, a = work(t)
        for number in range(4):
            pl.when(t == (0, 5, 14, 21)[number])(functools.partial(arrive, number))
        for number, first in ((1, 3), (2, 10), (3, 28)):
            pl.when(t == first)(functools.partial(turn, number))
        s = jnp.where(a % 2 == 1, (a + 1) // 2, jnp.where(a == 0, 0, 4 + a // 2))
        p = (z + jnp.where(s < 5, NZ - s, s - 4)) % NZ
        stat = jnp.zeros((8, 128), jnp.float32)
        for g in range(2):
            heads = slice(g * GROUP, (g + 1) * GROUP)
            qs = rbuf[pl.ds(8 * c, 8), pl.ds(2 * p, 2), heads, :].reshape(256, HD)
            ks = cache[s, 0, :, g * HD : (g + 1) * HD]
            vs = cache[s, 1, :, g * HD : (g + 1) * HD]
            sc = lax.dot_general(qs, ks, (((1,), (1,)), ((), ())), preferred_element_type=jnp.float32)
            top = jnp.max(sc, axis=1, keepdims=True)
            w = jnp.exp2((sc - top) * SCALE2).astype(jnp.bfloat16)
            o = jnp.dot(w, jnp.concatenate([vs, ones], axis=1), preferred_element_type=jnp.float32)
            total = o[:, HD:]
            res = (o[:, :HD] / total).astype(jnp.bfloat16)
            obuf[pl.ds(8 * c, 8), pl.ds(2 * p, 2), heads, :] = res.reshape(8, 2, GROUP, HD)
            lse = top * SCALE + jnp.log(total)
            spread = jnp.where(lane2 == spot2 + g * GROUP, lse, 0.0)
            stat = stat + jnp.sum(spread.reshape(8, 32, 128), axis=1)
        for n in range(8):
            stx[8 * c + n, pl.ds(p, 1), :] = stat[n : n + 1]
        return carry

    o_copies, s_copies = {}, {}
    lax.fori_loop(0, 28, step, 0)
    for number, chunk in enumerate(CHUNKS):
        lax.fori_loop(28 + number, 29 + number, step, 0)
        for n, i in enumerate(chunk):
            into = orx.at[0] if i == 0 else otx.at[i]

            def pack(j, carry, n=n, i=i, into=into):
                into[j] = obuf[8 * number + n, tab[i, 2 + row, base + j]]
                return carry

            lax.fori_loop(0, cap, pack, 0, unroll=True)
            if i == 0:
                srx[0] = stx[8 * number + n]
                continue
            copy = pltpu.make_async_remote_copy(
                src_ref=stx.at[8 * number + n], dst_ref=srx.at[i],
                send_sem=s_send.at[i], recv_sem=s_recv.at[i],
                device_id=other(i, -1), device_id_type=MESH,
            )
            copy.start()
            s_copies[i] = copy
            copy = pltpu.make_async_remote_copy(
                src_ref=otx.at[i], dst_ref=orx.at[i], send_sem=o_send.at[i], recv_sem=o_recv.at[i],
                device_id=other(i, -1), device_id_type=MESH,
            )
            copy.start()
            o_copies[i] = copy

    for copy in f_copies:
        copy.wait_recv()
    for dz in range(1, NZ):
        flags = jnp.maximum(flags, frx[dz - 1])
    over_ref[0] = jnp.max(flags[7:8, :].astype(jnp.float32))

    for chunk in CHUNKS:
        for i in chunk:
            if i:
                s_copies[i].wait_recv()
    for b in range(count // 8):
        rows = []
        for r in range(8 * b, 8 * b + 8):
            code = tab[0, 6, r]
            cell, slot = code // 256, code % 16
            pair = srx[2 * cell, pl.ds(slot // 2, 1), :] + srx[2 * cell + 1, pl.ds(slot // 2, 1), :]
            odd = jnp.full((1, 128), slot % 2, jnp.int32) == 1
            rows.append(jnp.where(odd, pltpu.roll(pair, 64, 1), pair))
        apad[8 * b : 8 * b + 8, :] = jnp.concatenate(rows, axis=0)
    share = 1.0 / (1.0 + jnp.exp(lses[...] - apad[0:count, :]))
    apad[0:count, :] = share
    apad[count:, :] = jnp.zeros((128 - count, 128), jnp.float32)
    turned = jnp.transpose(apad[...])
    for chunk in CHUNKS:
        for i in chunk:
            if i:
                o_copies[i].wait_recv()
    for r in range(count):
        code = tab[0, 6, r]
        cell, j = code // 256, code // 16 % 16
        pre = jnp.concatenate([orx[2 * cell + core, j], orx[2 * cell + 1 - core, j]], axis=0)
        mine = sufo[r]
        weight = jnp.broadcast_to(turned[:HQ, r : r + 1], (HQ, HD))
        out_ref[r] = (mine + weight * (pre.astype(jnp.float32) - mine)).astype(jnp.bfloat16)

    for swap in swaps:
        swap.wait_send()
    for pair in rings:
        for hops in pair:
            for hop in hops:
                hop.wait_send()
    for copy in f_copies:
        copy.wait_send()
    for group in (q_copies, m_copies, o_copies, s_copies):
        for copy in group.values():
            copy.wait_send()


def fused(cap, row_prefix, prefix_owner, suffix_len, missing, queries, suffix_kv, own_copy):
    count = queries.shape[0]
    smem = pl.BlockSpec(memory_space=pltpu.SMEM)
    vmem = pl.BlockSpec(memory_space=pltpu.VMEM)
    hbm = pl.BlockSpec(memory_space=pl.ANY)
    n = 2 * PLANE
    dma = pltpu.SemaphoreType.DMA
    bf16, f32 = jnp.bfloat16, jnp.float32
    return pl.pallas_call(
        functools.partial(fused_kernel, cap),
        out_shape=(
            jax.ShapeDtypeStruct((count, HQ, HD), bf16),
            jax.ShapeDtypeStruct((1,), f32),
        ),
        in_specs=[vmem, vmem, smem, smem, hbm, hbm, hbm],
        out_specs=(vmem, smem),
        scratch_shapes=[
            pltpu.VMEM((count, HQ, HD), bf16),
            pltpu.VMEM((count, 32, 1024), bf16),
            pltpu.VMEM((512, 1024), bf16),
            pltpu.VMEM((2, 512, 256), bf16),
            pltpu.VMEM((NZ, 2, 512, 256), bf16),
            pltpu.VMEM((n, cap, 32, HD), bf16),
            *[pltpu.VMEM((8, cap, 32, HD), bf16) for _ in CHUNKS],
            pltpu.VMEM((n, SLOTS, 32, HD), bf16),
            pltpu.VMEM((n, SLOTS, 32, HD), bf16),
            pltpu.VMEM((n, cap, 32, HD), bf16),
            pltpu.VMEM((n, cap, 32, HD), bf16),
            pltpu.VMEM((n, 8, 128), f32),
            pltpu.VMEM((n, 8, 128), f32),
            pltpu.VMEM((8, 128), jnp.int32),
            pltpu.VMEM((8, 128), jnp.int32),
            pltpu.VMEM((n, 8, 128), jnp.int32),
            pltpu.VMEM((8, 128), jnp.int32),
            pltpu.VMEM((NZ - 1, 8, 128), jnp.int32),
            pltpu.SMEM((n, 8, 128), jnp.int32),
            pltpu.VMEM((count, HQ, HD), f32),
            pltpu.VMEM((count, 128), f32),
            pltpu.VMEM((128, 128), f32),
            dma((3,)), dma((2,)), dma((2,)), dma((2, 4, 2)), dma((2, 4, 2)),
            dma((n,)), dma((n,)), dma((n,)), dma((n,)), dma((n,)),
            dma((n,)), dma((n,)), dma((n,)), dma((n,)), dma((NZ - 1,)), dma((NZ - 1,)),
        ],
        compiler_params=pltpu.CompilerParams(
            collective_id=cap, has_side_effects=True, vmem_limit_bytes=58 * 2**20
        ),
    )(row_prefix, prefix_owner, suffix_len, missing, queries, suffix_kv, own_copy)


CAP = 12


def body(queries, suffix_kv, suffix_len, row_prefix, prefix_owner, prefix_kv, missing_pages):
    count, width = queries.shape
    args = (
        row_prefix.reshape(1, count), prefix_owner.reshape(1, -1), suffix_len, missing_pages[0, 0],
        queries.reshape(count, HQ, HD), suffix_kv, prefix_kv[0, 0],
    )
    quick, over = fused(CAP, *args)
    return lax.cond(
        over[0] > 0.5,
        lambda: fused(SLOTS, *args)[0].reshape(count, width),
        lambda: quick.reshape(count, width),
    )


def solution(mesh):
    in_specs = (
        P(("owner", "replica"), None),
        P(("owner", "replica"), None, None),
        P(("owner", "replica")),
        P(("owner", "replica"), None),
        P(),
        P("owner", "replica", None, None),
        P("owner", None, None),
    )
    out_specs = P(("owner", "replica"), None)
    return jax.shard_map(body, mesh=mesh, in_specs=in_specs, out_specs=out_specs, check_vma=False)
```

```python
import functools

import jax
import jax.numpy as jnp
from jax import lax
from jax.experimental import pallas as pl
from jax.experimental.pallas import tpu as pltpu
from jax.sharding import PartitionSpec as P

HQ = 64
KVH = 4
HD = 128
PAGE = 128
GROUP = HQ // KVH
NZ, NY, NX = 8, 4, 4
PLANE = NY * NX
SLOTS = 2 * NZ
SCALE = HD**-0.5
SCALE2 = SCALE * 1.4426950408889634
MESH = pl.DeviceIdType.MESH

ORDER = (
    ((0, 0), (1, 1), (3, 3), (1, 3)),
    ((3, 1), (2, 1), (1, 2), (1, 0)),
    ((3, 0), (0, 1), (0, 3), (2, 0)),
    ((0, 2), (2, 3), (3, 2), (2, 2)),
)
CHUNKS = tuple(
    tuple(2 * (dy * NX + dx) + hh for dx, dy in chunk for hh in (0, 1)) for chunk in ORDER
)
PLACE = {i: (c, n) for c, chunk in enumerate(CHUNKS) for n, i in enumerate(chunk)}


PLAN = (
    0, (0, 0, 3), 1, (0, 3, 5), (1, 0, 5), 2, (0, 5, 7), (1, 5, 7), 3,
    (0, 7, 8), (1, 7, 8), (2, 0, 8), (3, 0, 8),
)
RUNS, HOPS, ARRIVALS, ENDS = [], {}, {}, {}
for entry in PLAN:
    first = RUNS[-1][1] if RUNS else 0
    if isinstance(entry, int):
        HOPS[entry] = first
    else:
        RUNS.append((first, first + entry[2] - entry[1], entry[0], entry[1]))
        ARRIVALS.setdefault(entry[0], first)
        ENDS[entry[0]] = RUNS[-1][1]


def work(t):
    chunk, place = jnp.int32(0), jnp.int32(0)
    for first, end, number, start in RUNS:
        inside = (t >= first) & (t < end)
        chunk = jnp.where(inside, number, chunk)
        place = jnp.where(inside, t - first + start, place)
    return chunk, place


def fused_kernel(
    cap,
    pre_ref, own_ref, len_ref, miss_ref, q_hbm, suf_hbm, kv_hbm,
    out_ref, over_ref,
    q, suf, kv, kvp, cache, tx, rx0, rx1, rx2, rx3, rbuf, obuf, otx, orx, stx, srx,
    rows_v, tab_v, mrx, flag_v, frx, tab, sufo, lses, apad,
    in_sem, core_send, core_recv, z_send, z_recv,
    q_send, q_recv, m_send, m_recv, tab_sem, o_send, o_recv, s_send, s_recv,
    f_send, f_recv,
):
    own = lax.axis_index("owner")
    core = lax.axis_index("replica")
    rx = (rx0, rx1, rx2, rx3)
    z, y, x = own // PLANE, own // NX % NY, own % NX
    here = own % PLANE

    def plane(dx, dy):
        return ((y + dy) % NY) * NX + (x + dx) % NX

    def other(i, sign):
        cell, hh = i // 2, i % 2
        dx, dy = cell % NX, cell // NX
        spot = z * PLANE + plane(sign * dx + NX, sign * dy + NY)
        return spot, (1 - core if hh else core)

    load_kv = pltpu.make_async_copy(kv_hbm, kv, in_sem.at[0])
    load_q = pltpu.make_async_copy(q_hbm, q, in_sem.at[1])
    load_suf = pltpu.make_async_copy(suf_hbm, suf, in_sem.at[2])
    load_kv.start()
    load_q.start()

    z_up = (z + 1) % NZ * PLANE + here
    z_down = (z + NZ - 1) % NZ * PLANE + here
    barrier = pltpu.get_barrier_semaphore()
    for i in range(1, 2 * PLANE):
        pl.semaphore_signal(barrier, inc=1, device_id=other(i, 1), device_id_type=MESH)
    for dz in range(1, NZ):
        level = ((z + dz) % NZ * PLANE + here, core)
        pl.semaphore_signal(barrier, inc=1, device_id=level, device_id_type=MESH)

    lane = lax.broadcasted_iota(jnp.int32, (128, 128), 1)
    sub = lax.broadcasted_iota(jnp.int32, (128, 128), 0)

    def down(row):
        return jnp.transpose(jnp.broadcast_to(row, (128, 128)))

    def pick(mask, value):
        return jnp.sum(jnp.where(mask, value, 0), axis=0, keepdims=True)

    count = pre_ref.shape[1]
    rows_v[...] = jnp.full((8, 128), -1, jnp.int32)
    rows_v[0:1, 0:count] = pre_ref[...]
    real = lane[0:1] < count
    owner = pick(sub == rows_v[0:1, :], down(own_ref[...]))
    spot = jnp.where(real, owner & 15, 99)
    owner = jnp.where(real, owner, 999)
    earlier = sub < lane
    repeat = pick((down(owner) == owner) & earlier, 1)
    slot = jnp.minimum((owner >> 4) * 2 + repeat, SLOTS - 1)
    rank = pick((down(spot) == spot) & earlier, 1)
    kept = jnp.minimum(rank, cap - 1)
    by_rank, by_slot = down(spot * 16 + rank), down(spot * 16 + slot)
    slot_down, kept_down = down(slot), down(kept)
    for half in range(2):
        keys = lane + 128 * half
        tab_v[half : half + 1, :] = jnp.minimum(pick(by_rank == keys, sub), count - 1)
        tab_v[2 + half : 3 + half, :] = jnp.minimum(pick(by_rank == keys, slot_down), SLOTS - 1)
        tab_v[4 + half : 5 + half, :] = jnp.minimum(pick(by_slot == keys, kept_down), cap - 1)
    cell = (((spot >> 2) - y) & 3) * 4 + (((spot & 3) - x) & 3)
    tab_v[6:7, :] = cell * 256 + kept * 16 + slot
    tab_v[7:8, :] = jnp.where(real & (rank >= cap), 1, 0)
    load_tab = pltpu.make_async_copy(tab_v, tab.at[0], tab_sem.at[0])
    load_tab.start()
    load_kv.wait()
    pl.semaphore_wait(barrier, 2 * PLANE + NZ - 2)

    swaps = []
    for part in range(2):
        lanes = pl.ds(pl.multiple_of(part * 512 + (1 - core) * 256, 256), 256)
        swap = pltpu.make_async_remote_copy(
            src_ref=kv.at[:, lanes], dst_ref=kvp.at[part],
            send_sem=core_send.at[part], recv_sem=core_recv.at[part],
            device_id=(own, 1 - core), device_id_type=MESH,
        )
        swap.start()
        swaps.append(swap)

    q_copies, m_copies = {}, {}

    def send_table(i):
        copy = pltpu.make_async_remote_copy(
            src_ref=tab_v, dst_ref=mrx.at[i], send_sem=m_send.at[i], recv_sem=m_recv.at[i],
            device_id=other(i, 1), device_id_type=MESH,
        )
        copy.start()
        m_copies[i] = copy

    def send_queries(i):
        cell, hh = i // 2, i % 2
        dest = plane(cell % NX, cell // NX)
        first = pl.multiple_of((1 - core if hh else core) * 32, 32)
        arrive = rx[PLACE[i][0]].at[PLACE[i][1]]
        into = arrive if i == 0 else tx.at[i]

        def put(j, carry):
            into[j] = q[tab[0, dest // 8, dest % 8 * 16 + j], pl.ds(first, 32), :]
            return carry

        lax.fori_loop(0, cap, put, 0, unroll=True)
        if i == 0:
            return
        copy = pltpu.make_async_remote_copy(
            src_ref=tx.at[i], dst_ref=arrive,
            send_sem=q_send.at[i], recv_sem=q_recv.at[i],
            device_id=other(i, 1), device_id_type=MESH,
        )
        copy.start()
        q_copies[i] = copy

    for i in range(1, 2 * PLANE):
        send_table(i)
    load_q.wait()
    load_suf.start()
    load_tab.wait()

    def ring(step, up, part):
        if step < 3:
            src = cache.at[step if up or step == 0 else 4 + step, part]
            dst = cache.at[step + 1 if up else 5 + step, part]
        else:
            src, dst = cache.at[3 if up else 7, part], cache.at[4, part]
        way = 0 if up else 1
        return pltpu.make_async_remote_copy(
            src_ref=src, dst_ref=dst,
            send_sem=z_send.at[way, step, part], recv_sem=z_recv.at[way, step, part],
            device_id=(z_up if up else z_down, core), device_id_type=MESH,
        )

    rings = [
        [[ring(step, up, part) for up in (True, False) if step < 3 or up == (part == 0)] for part in range(2)]
        for step in range(4)
    ]

    def turn(step):
        for part in range(2):
            for hop in rings[step][part]:
                hop.wait_recv()
            if step < 3:
                for hop in rings[step + 1][part]:
                    hop.start()

    for part in range(2):
        swaps[part].wait_recv()
        lanes = pl.ds(pl.multiple_of(part * 512 + core * 256, 256), 256)
        for page in range(4):
            rows = slice(page * PAGE, (page + 1) * PAGE)
            take = jnp.where(page == miss_ref[0], 1 - core, core)
            pick_it = jnp.full((PAGE, 256), take, jnp.int32) == 1
            cache[0, part, rows, :] = jnp.where(pick_it, kvp[part, rows, :], kv[rows, lanes])
        for hop in rings[0][part]:
            hop.start()
    for chunk in CHUNKS:
        for i in chunk:
            send_queries(i)

    load_suf.wait()

    def suffix_block(b, carry):
        col = lax.broadcasted_iota(jnp.int32, (GROUP, 256), 1)
        valid = jnp.concatenate(
            [(col >= 32 * n) & (col < 32 * n + len_ref[b * 8 + n]) for n in range(8)], axis=0
        )
        head = sub % GROUP
        rows = pl.ds(b * 8, 8)
        stat = jnp.zeros((8, 128), jnp.float32)
        ones = jnp.ones((256, 128), jnp.bfloat16)
        for g in range(KVH):
            qs = q[rows, g * GROUP : (g + 1) * GROUP, :].reshape(128, HD)
            ks = suf[rows, :, g * HD : (g + 1) * HD].reshape(256, HD)
            vs = suf[rows, :, 512 + g * HD : 512 + (g + 1) * HD].reshape(256, HD)
            s = lax.dot_general(qs, ks, (((1,), (1,)), ((), ())), preferred_element_type=jnp.float32)
            s = jnp.where(valid, s, -3e38)
            top = jnp.max(s, axis=1, keepdims=True)
            w = jnp.exp2((s - top) * SCALE2).astype(jnp.bfloat16)
            o = jnp.dot(w, jnp.concatenate([vs, ones], axis=1), preferred_element_type=jnp.float32)
            total = o[:, HD:]
            sufo[rows, g * GROUP : (g + 1) * GROUP, :] = (o[:, :HD] / total).reshape(8, GROUP, HD)
            lse = top * SCALE + jnp.log(total)
            spread = jnp.where(lane == g * GROUP + head, lse, 0.0)
            stat = stat + jnp.sum(spread.reshape(8, GROUP, 128), axis=1)
        lses[pl.ds(pl.multiple_of(b * 8, 8), 8), :] = stat
        return carry

    lax.fori_loop(0, count // 8, suffix_block, 0)

    base, row = here % 8 * 16, here // 8
    ones = jnp.ones((512, 128), jnp.bfloat16)
    lane2 = lax.broadcasted_iota(jnp.int32, (256, 128), 1)
    within = lax.broadcasted_iota(jnp.int32, (256, 128), 0) % 32
    spot2 = within // GROUP * 64 + core * 32 + within % GROUP

    def arrive(number):
        chunk = CHUNKS[number]
        tabs = []
        for i in chunk:
            if i:
                m_copies[i].wait_recv()
                fetch = pltpu.make_async_copy(mrx.at[i], tab.at[i], tab_sem.at[i])
                fetch.start()
                tabs.append(fetch)
        for i in chunk:
            if i:
                q_copies[i].wait_recv()
        for fetch in tabs:
            fetch.wait()
        for n, i in enumerate(chunk):

            def spread_out(s, carry, n=n, i=i):
                rbuf[8 * number + n, s] = rx[number][n, tab[i, 4 + row, base + s]]
                return carry

            lax.fori_loop(0, SLOTS, spread_out, 0, unroll=True)

    def step(t, carry):
        c, a = work(t)
        for number in range(4):
            pl.when(t == HOPS[number])(functools.partial(turn, number))
        for number in range(4):
            pl.when(t == ARRIVALS[number])(functools.partial(arrive, number))
        s = jnp.where(a % 2 == 1, (a + 1) // 2, jnp.where(a == 0, 0, 4 + a // 2))
        p = (z + jnp.where(s < 5, NZ - s, s - 4)) % NZ
        stat = jnp.zeros((8, 128), jnp.float32)
        for g in range(2):
            heads = slice(g * GROUP, (g + 1) * GROUP)
            qs = rbuf[pl.ds(8 * c, 8), pl.ds(2 * p, 2), heads, :].reshape(256, HD)
            ks = cache[s, 0, :, g * HD : (g + 1) * HD]
            vs = cache[s, 1, :, g * HD : (g + 1) * HD]
            sc = lax.dot_general(qs, ks, (((1,), (1,)), ((), ())), preferred_element_type=jnp.float32)
            top = jnp.max(sc, axis=1, keepdims=True)
            w = jnp.exp2((sc - top) * SCALE2).astype(jnp.bfloat16)
            o = jnp.dot(w, jnp.concatenate([vs, ones], axis=1), preferred_element_type=jnp.float32)
            total = o[:, HD:]
            res = (o[:, :HD] / total).astype(jnp.bfloat16)
            obuf[pl.ds(8 * c, 8), pl.ds(2 * p, 2), heads, :] = res.reshape(8, 2, GROUP, HD)
            lse = top * SCALE + jnp.log(total)
            spread = jnp.where(lane2 == spot2 + g * GROUP, lse, 0.0)
            stat = stat + jnp.sum(spread.reshape(8, 32, 128), axis=1)
        for n in range(8):
            stx[8 * c + n, pl.ds(p, 1), :] = stat[n : n + 1]
        return carry

    o_copies, s_copies, f_copies = {}, {}, []
    done = 0
    for number, chunk in enumerate(CHUNKS):
        lax.fori_loop(done, ENDS[number], step, 0)
        done = ENDS[number]
        for n, i in enumerate(chunk):
            into = orx.at[0] if i == 0 else otx.at[i]

            def pack(j, carry, n=n, i=i, into=into):
                into[j] = obuf[8 * number + n, tab[i, 2 + row, base + j]]
                return carry

            lax.fori_loop(0, cap, pack, 0, unroll=True)
            if i == 0:
                srx[0] = stx[8 * number + n]
                continue
            copy = pltpu.make_async_remote_copy(
                src_ref=stx.at[8 * number + n], dst_ref=srx.at[i],
                send_sem=s_send.at[i], recv_sem=s_recv.at[i],
                device_id=other(i, -1), device_id_type=MESH,
            )
            copy.start()
            s_copies[i] = copy
            copy = pltpu.make_async_remote_copy(
                src_ref=otx.at[i], dst_ref=orx.at[i], send_sem=o_send.at[i], recv_sem=o_recv.at[i],
                device_id=other(i, -1), device_id_type=MESH,
            )
            copy.start()
            o_copies[i] = copy
        if number < len(CHUNKS) - 1:
            continue

        flags = tab_v[...]
        for i in range(1, 2 * PLANE):
            flags = jnp.maximum(flags, mrx[i])
        flag_v[...] = flags
        for dz in range(1, NZ):
            copy = pltpu.make_async_remote_copy(
                src_ref=flag_v, dst_ref=frx.at[dz - 1], send_sem=f_send.at[dz - 1], recv_sem=f_recv.at[dz - 1],
                device_id=((z + dz) % NZ * PLANE + here, core), device_id_type=MESH,
            )
            copy.start()
            f_copies.append(copy)

    for copy in f_copies:
        copy.wait_recv()
    for dz in range(1, NZ):
        flags = jnp.maximum(flags, frx[dz - 1])
    over_ref[0] = jnp.max(flags[7:8, :].astype(jnp.float32))

    for chunk in CHUNKS:
        for i in chunk:
            if i:
                s_copies[i].wait_recv()
    for b in range(count // 8):
        rows = []
        for r in range(8 * b, 8 * b + 8):
            code = tab[0, 6, r]
            cell, slot = code // 256, code % 16
            pair = srx[2 * cell, pl.ds(slot // 2, 1), :] + srx[2 * cell + 1, pl.ds(slot // 2, 1), :]
            odd = jnp.full((1, 128), slot % 2, jnp.int32) == 1
            rows.append(jnp.where(odd, pltpu.roll(pair, 64, 1), pair))
        apad[8 * b : 8 * b + 8, :] = jnp.concatenate(rows, axis=0)
    share = 1.0 / (1.0 + jnp.exp(lses[...] - apad[0:count, :]))
    apad[0:count, :] = share
    apad[count:, :] = jnp.zeros((128 - count, 128), jnp.float32)
    turned = jnp.transpose(apad[...])
    for chunk in CHUNKS:
        for i in chunk:
            if i:
                o_copies[i].wait_recv()
    for r in range(count):
        code = tab[0, 6, r]
        cell, j = code // 256, code // 16 % 16
        pre = jnp.concatenate([orx[2 * cell + core, j], orx[2 * cell + 1 - core, j]], axis=0)
        mine = sufo[r]
        weight = jnp.broadcast_to(turned[:HQ, r : r + 1], (HQ, HD))
        out_ref[r] = (mine + weight * (pre.astype(jnp.float32) - mine)).astype(jnp.bfloat16)

    for swap in swaps:
        swap.wait_send()
    for pair in rings:
        for hops in pair:
            for hop in hops:
                hop.wait_send()
    for copy in f_copies:
        copy.wait_send()
    for group in (q_copies, m_copies, o_copies, s_copies):
        for copy in group.values():
            copy.wait_send()


def fused(cap, row_prefix, prefix_owner, suffix_len, missing, queries, suffix_kv, own_copy):
    count = queries.shape[0]
    smem = pl.BlockSpec(memory_space=pltpu.SMEM)
    vmem = pl.BlockSpec(memory_space=pltpu.VMEM)
    hbm = pl.BlockSpec(memory_space=pl.ANY)
    n = 2 * PLANE
    dma = pltpu.SemaphoreType.DMA
    bf16, f32 = jnp.bfloat16, jnp.float32
    return pl.pallas_call(
        functools.partial(fused_kernel, cap),
        out_shape=(
            jax.ShapeDtypeStruct((count, HQ, HD), bf16),
            jax.ShapeDtypeStruct((1,), f32),
        ),
        in_specs=[vmem, vmem, smem, smem, hbm, hbm, hbm],
        out_specs=(vmem, smem),
        scratch_shapes=[
            pltpu.VMEM((count, HQ, HD), bf16),
            pltpu.VMEM((count, 32, 1024), bf16),
            pltpu.VMEM((512, 1024), bf16),
            pltpu.VMEM((2, 512, 256), bf16),
            pltpu.VMEM((NZ, 2, 512, 256), bf16),
            pltpu.VMEM((n, cap, 32, HD), bf16),
            *[pltpu.VMEM((8, cap, 32, HD), bf16) for _ in CHUNKS],
            pltpu.VMEM((n, SLOTS, 32, HD), bf16),
            pltpu.VMEM((n, SLOTS, 32, HD), bf16),
            pltpu.VMEM((n, cap, 32, HD), bf16),
            pltpu.VMEM((n, cap, 32, HD), bf16),
            pltpu.VMEM((n, 8, 128), f32),
            pltpu.VMEM((n, 8, 128), f32),
            pltpu.VMEM((8, 128), jnp.int32),
            pltpu.VMEM((8, 128), jnp.int32),
            pltpu.VMEM((n, 8, 128), jnp.int32),
            pltpu.VMEM((8, 128), jnp.int32),
            pltpu.VMEM((NZ - 1, 8, 128), jnp.int32),
            pltpu.SMEM((n, 8, 128), jnp.int32),
            pltpu.VMEM((count, HQ, HD), f32),
            pltpu.VMEM((count, 128), f32),
            pltpu.VMEM((128, 128), f32),
            dma((3,)), dma((2,)), dma((2,)), dma((2, 4, 2)), dma((2, 4, 2)),
            dma((n,)), dma((n,)), dma((n,)), dma((n,)), dma((n,)),
            dma((n,)), dma((n,)), dma((n,)), dma((n,)), dma((NZ - 1,)), dma((NZ - 1,)),
        ],
        compiler_params=pltpu.CompilerParams(
            collective_id=cap, has_side_effects=True, vmem_limit_bytes=58 * 2**20
        ),
    )(row_prefix, prefix_owner, suffix_len, missing, queries, suffix_kv, own_copy)


CAP = 11


def body(queries, suffix_kv, suffix_len, row_prefix, prefix_owner, prefix_kv, missing_pages):
    count, width = queries.shape
    args = (
        row_prefix.reshape(1, count), prefix_owner.reshape(1, -1), suffix_len, missing_pages[0, 0],
        queries.reshape(count, HQ, HD), suffix_kv, prefix_kv[0, 0],
    )
    quick, over = fused(CAP, *args)
    return lax.cond(
        over[0] > 0.5,
        lambda: fused(SLOTS, *args)[0].reshape(count, width),
        lambda: quick.reshape(count, width),
    )


def solution(mesh):
    in_specs = (
        P(("owner", "replica"), None),
        P(("owner", "replica"), None, None),
        P(("owner", "replica")),
        P(("owner", "replica"), None),
        P(),
        P("owner", "replica", None, None),
        P("owner", None, None),
    )
    out_specs = P(("owner", "replica"), None)
    return jax.shard_map(body, mesh=mesh, in_specs=in_specs, out_specs=out_specs, check_vma=False)
```
